512 devices in a mesh: dp: 16 (over y, x_hi, core), ctx: 32 (over z, x_lo).
Axes of the slice: x: 4 (x_hi: 2, x_lo: 2; x = x_hi * 2 + x_lo), y: 4, z: 16, core: 2. Of those that a mesh axis runs over, the one named last changes fastest.
Arguments:
- out_gate: bfloat16 [16, 8192, 512], P('dp', 'ctx'), may hold values from -6 to 6
- key_gate: bfloat16 [16, 8192, 512], P('dp', 'ctx'), may hold values from -6 to 6
- value_input: bfloat16 [16, 8192, 512], P('dp', 'ctx'), may hold values from -6 to 6
- filter_taps: bfloat16 [8192, 512], P('ctx'), may hold values from -2 to 2
- cotangent: bfloat16 [16, 8192, 512], P('dp', 'ctx'), may hold values from -6 to 6
- block_live: int32 [16, 128], P('dp', 'ctx'), may hold values 0 or 1
Outputs:
- grad_out_gate: bfloat16 [16, 8192, 512], P('dp', 'ctx')
- grad_key_gate: bfloat16 [16, 8192, 512], P('dp', 'ctx')
- grad_value: bfloat16 [16, 8192, 512], P('dp', 'ctx')
- grad_taps: bfloat16 [8192, 512], P('ctx')
The draws below stay inside these ranges and needn't reach their ends.
Inputs may be any that keep to these rules, and one draw needn't show every extreme that they name: `block_live`: 1 where a block of 64 tokens holds sequence data, 0 where it is padding.
All inputs are finite; a program needn't handle non-finite values.
Results may differ from the reference program's by a relative error of at most 0.027.
Values may be sent and summed in bfloat16 or wider, within the bound.
A program may use at most 64 MiB of HBM per device.

```python
import math
import jax
import jax.numpy as jnp
from jax import lax

CH = 512
QLEN = 64
BLOCK = 64
SEQ = 8192
PLEN = 256
BATCH = 16


def draw_filter_taps(key, part):
    rate_key, noise_key = jax.random.split(key)
    lowest = math.log(0.3)
    highest = math.log(SEQ / 30.0)
    decay_rates = jnp.exp(jax.random.uniform(rate_key, (1, CH), jnp.float32, lowest, highest))
    positions = jnp.arange(SEQ, dtype=jnp.float32)[:, None]
    envelope = jnp.exp(-decay_rates * positions / SEQ)
    energy = jnp.expm1(-2.0 * decay_rates) / jnp.expm1(-2.0 * decay_rates / SEQ)
    noise_vals = jnp.clip(jax.random.normal(noise_key, (SEQ, CH), jnp.float32), -6.0, 6.0)
    return (noise_vals * envelope / jnp.sqrt(energy)).astype(jnp.bfloat16)


def set_ends(entries, own_key, smallest, high):
    longest = entries.shape.index(max(entries.shape))
    spots = []
    for shift in (0, 1):
        where = [jax.random.randint(jax.random.fold_in(own_key, axis), (), 0, length) for axis, length in enumerate(entries.shape)]
        where[longest] = (where[longest] + shift) % entries.shape[longest]
        spots.append(tuple(where))
    return entries.at[spots[0]].set(smallest).at[spots[1]].set(high)


def block_levels(rng, extent, cuts, low, top_value):
    def one(dim, parts):
        steps = jax.random.uniform(jax.random.fold_in(jax.random.fold_in(rng, 6), dim), (parts,), jnp.float32, low / len(cuts), top_value / len(cuts))
        return jnp.repeat(jnp.exp(steps), extent[dim] // parts).reshape((-1,) + (1,) * (len(extent) - dim - 1))

    loudness = one(*cuts[0])
    for cut in cuts[1:]:
        loudness = loudness * one(*cut)
    return loudness


def normal_values(own_key, shape, deviation, most, shards=(), held_as=jnp.bfloat16):
    level = block_levels(own_key, shape, shards, -0.22, 0.18) if shards else 1.0
    result = jax.random.normal(own_key, shape, jnp.float32) * deviation * level
    return jnp.minimum(jnp.maximum(result, -most), most).astype(held_as)


def setup_inputs(seed: int = 0) -> dict:
    key_of = jax.random.split(jax.random.key(seed), 7)
    return {
        "out_gate": normal_values(key_of[0], (BATCH, SEQ, CH), 1.0, 6.0, ((0, 16), (1, 32))),
        "key_gate": normal_values(key_of[1], (BATCH, SEQ, CH), 1.0, 6.0, ((0, 16), (1, 32))),
        "value_input": normal_values(key_of[2], (BATCH, SEQ, CH), 1.0, 6.0, ((0, 16), (1, 32))),
        "filter_taps": draw_filter_taps(jax.random.fold_in(key_of[6], 71), 0),
        "cotangent": normal_values(key_of[4], (BATCH, SEQ, CH), 1.0, 6.0, ((0, 16), (1, 32))),
        "block_live": set_ends((jax.random.randint(key_of[5], (BATCH, SEQ // BLOCK), 0, 4) < 3).astype(jnp.int32), jax.random.fold_in(key_of[5], 1), 0, 1),
    }


TWO_PI = 2.0 * math.pi

def angle_table(row_count, col_count, row_start, col_start, period_len, direction):
    row_ids = jnp.arange(row_count, dtype=jnp.int32)[:, None] + row_start
    col_ids = jnp.arange(col_count, dtype=jnp.int32)[None, :] + col_start
    phases = (row_ids * col_ids % period_len).astype(jnp.float32)
    return direction * TWO_PI * phases / period_len

def rounded(values):
    return lax.optimization_barrier(values.astype(jnp.bfloat16)).astype(jnp.float32)

def factor_tables(angles):
    return (rounded(jnp.cos(angles)), rounded(jnp.sin(angles)))

def product(form, left_op, right_op):
    return jnp.einsum(form, left_op, right_op, precision=lax.Precision.HIGHEST)

def forward_full(signal):
    half_rows = PLEN // 2
    total_len = PLEN * QLEN
    grid_values = signal.astype(jnp.float32).reshape(half_rows, QLEN, CH)
    cos_rows, sin_rows = factor_tables(angle_table(PLEN, half_rows, 0, 0, PLEN, -1.0))
    real_part = product('kp,pqc->kqc', cos_rows, grid_values)
    imag_part = product('kp,pqc->kqc', sin_rows, grid_values)
    twist_angles = angle_table(PLEN, QLEN, 0, 0, total_len, -1.0)
    turn_cos = jnp.cos(twist_angles)[:, :, None]
    turn_sin = jnp.sin(twist_angles)[:, :, None]
    real_twist = rounded(real_part * turn_cos - imag_part * turn_sin)
    imag_twist = rounded(real_part * turn_sin + imag_part * turn_cos)
    cos_cols, sin_cols = factor_tables(angle_table(QLEN, QLEN, 0, 0, QLEN, -1.0))
    real_out = product('aqc,qk->akc', real_twist, cos_cols) - product('aqc,qk->akc', imag_twist, sin_cols)
    imag_out = product('aqc,qk->akc', real_twist, sin_cols) + product('aqc,qk->akc', imag_twist, cos_cols)
    return (rounded(real_out), rounded(imag_out))

def inverse_full(real_in, imag_in):
    total_len = PLEN * QLEN
    cos_cols, sin_cols = factor_tables(angle_table(QLEN, QLEN, 0, 0, QLEN, 1.0))
    real_part = product('akc,kq->aqc', real_in, cos_cols) - product('akc,kq->aqc', imag_in, sin_cols)
    imag_part = product('akc,kq->aqc', real_in, sin_cols) + product('akc,kq->aqc', imag_in, cos_cols)
    twist_angles = angle_table(PLEN, QLEN, 0, 0, total_len, 1.0)
    turn_cos = jnp.cos(twist_angles)[:, :, None]
    turn_sin = jnp.sin(twist_angles)[:, :, None]
    real_twist = rounded(real_part * turn_cos - imag_part * turn_sin)
    imag_twist = rounded(real_part * turn_sin + imag_part * turn_cos)
    cos_back, sin_back = factor_tables(angle_table(PLEN // 2, PLEN, 0, 0, PLEN, 1.0))
    signal = product('pk,kqc->pqc', cos_back, real_twist) - product('pk,kqc->pqc', sin_back, imag_twist)
    return (signal * (1.0 / total_len)).astype(jnp.bfloat16).reshape(SEQ, CH)

def spectrum_product(left_real, left_imag, right_real, right_imag, conjugate):
    if conjugate:
        real_out = left_real * right_real + left_imag * right_imag
        imag_out = left_imag * right_real - left_real * right_imag
    else:
        real_out = left_real * right_real - left_imag * right_imag
        imag_out = left_real * right_imag + left_imag * right_real
    return (rounded(real_out), rounded(imag_out))

def reference(out_gate, key_gate, value_input, filter_taps, cotangent, block_live):
    filter_real, filter_imag = forward_full(filter_taps)
    live_tokens = jnp.repeat(block_live.astype(jnp.float32), BLOCK, axis=1)[:, :, None]

    def one_sequence(taps_total, row_items):
        gate_row, key_row, value_row, cot_row, live_row = row_items
        key_wide = key_row.astype(jnp.float32)
        value_wide = value_row.astype(jnp.float32)
        cot_wide = cot_row.astype(jnp.float32)
        gated_input = (key_wide * value_wide * live_row).astype(jnp.bfloat16)
        back_signal = (cot_wide * gate_row.astype(jnp.float32)).astype(jnp.bfloat16)
        fwd_real, fwd_imag = forward_full(gated_input)
        back_real, back_imag = forward_full(back_signal)
        conv_real, conv_imag = spectrum_product(fwd_real, fwd_imag, filter_real, filter_imag, False)
        conv_out = inverse_full(conv_real, conv_imag)
        grad_real, grad_imag = spectrum_product(back_real, back_imag, filter_real, filter_imag, True)
        grad_conv = inverse_full(grad_real, grad_imag)
        taps_real, taps_imag = spectrum_product(back_real, back_imag, fwd_real, fwd_imag, True)
        taps_seq = inverse_full(taps_real, taps_imag)
        grad_gate = (cot_wide * conv_out.astype(jnp.float32)).astype(jnp.bfloat16)
        grad_wide = grad_conv.astype(jnp.float32)
        grad_key = (grad_wide * value_wide * live_row).astype(jnp.bfloat16)
        grad_value = (grad_wide * key_wide * live_row).astype(jnp.bfloat16)
        return (taps_total + taps_seq.astype(jnp.float32), (grad_gate, grad_key, grad_value))
    taps_total, grad_rows = lax.scan(one_sequence, jnp.zeros((SEQ, CH), jnp.float32), (out_gate, key_gate, value_input, cotangent, live_tokens))
    grad_taps = (taps_total * (1.0 / math.sqrt(BATCH * SEQ))).astype(jnp.bfloat16)
    return (grad_rows[0], grad_rows[1], grad_rows[2], grad_taps)
```

```python
import functools
import math

import jax
import jax.numpy as jnp
import ml_dtypes
import numpy as np
from jax import lax
from jax.experimental import pallas as pl
from jax.experimental.pallas import tpu as pltpu
from jax.sharding import PartitionSpec as P

MESH = pl.DeviceIdType.MESH
F32 = jnp.float32
BF16 = jnp.bfloat16


@functools.lru_cache(maxsize=None)
def tables(parts, length, group):
    full = 2 * parts
    low = np.arange(parts + 1)
    block = np.arange(parts)
    step = np.arange(length)
    turn = 2.0 * np.pi / full * (low[:, None] * block[None, :] % full)
    eye = np.eye(group)
    spread = lambda m: np.kron(m, eye)
    cos1, sin1 = np.cos(turn), np.sin(turn)
    first = np.concatenate([spread(cos1), spread(-sin1[1:parts])], axis=0)
    weight = np.full((parts + 1, 1), 2.0)
    weight[0] = weight[parts] = 1.0
    last = np.concatenate([spread((weight * cos1).T), spread((-weight * sin1)[1:parts].T)], axis=1)
    cols = 2.0 * np.pi / length * (step[:, None] * step[None, :] % length)
    cos2, sin2 = np.cos(cols), np.sin(cols)
    fwd = np.block([[cos2, -sin2], [sin2, cos2]])
    inv = np.block([[cos2, sin2], [-sin2, cos2]])
    twist = 2.0 * np.pi / (full * length) * (low[:, None] * step[None, :])
    rows = lambda m: np.repeat(m[:, None, :], 8, axis=1).astype(np.float32)
    half = lambda m: m.astype(np.float32).astype(ml_dtypes.bfloat16)
    return (half(first), half(fwd), half(inv), half(last), rows(np.cos(twist)), rows(np.sin(twist)))


def kernel(
    devices,
    live,
    key_hbm,
    val_hbm,
    taps_hbm,
    cot_hbm,
    gate_hbm,
    first_hbm,
    fwd_hbm,
    inv_hbm,
    last_hbm,
    tcos_hbm,
    tsin_hbm,
    out_gate,
    out_key,
    out_val,
    out_taps,
    key,
    val,
    taps,
    cot,
    gate,
    first,
    fwd,
    inv,
    last,
    tcos,
    tsin,
    gated_s,
    back_s,
    filt_s,
    gated_r,
    back_r,
    filt_r,
    conv_s,
    grad_s,
    taps_s,
    conv_r,
    grad_r,
    sums_r,
    total,
    taps_r,
    spec_f,
    spec_b,
    spec_h,
    twisted,
    load_sem,
    send_sem,
    recv_sem,
    small_sem,
):
    n_dp, n_ctx = devices
    n_z = n_ctx // 2
    d = lax.axis_index("dp")
    c = lax.axis_index("ctx")
    z, x = c // 2, c % 2
    chans, length = n_ctx * gated_s.shape[1], gated_s.shape[2]
    group = gated_s.shape[1]
    n_low = n_ctx + 1
    blocks = live.shape[1]
    block = length // blocks

    def shift_of(place):
        pair, core = place // 2, place % 2
        return pair + core * (n_dp - 2 * pair - (n_dp // 2) * ((n_dp - pair) // n_dp))

    shift = shift_of(d)
    pair_in = (z + shift) % n_z
    pair_out = (z - shift + n_z) % n_z

    loads = [
        pltpu.make_async_copy(src, dst, load_sem.at[i])
        for i, (src, dst) in enumerate(
            [
                (taps_hbm, taps),
                (key_hbm, key),
                (val_hbm, val),
                (cot_hbm, cot),
                (gate_hbm, gate),
                (first_hbm, first),
                (tcos_hbm, tcos),
                (tsin_hbm, tsin),
                (fwd_hbm, fwd),
                (inv_hbm, inv),
                (last_hbm, last),
            ]
        )
    ]
    for load in loads:
        load.start()

    barrier = pltpu.get_barrier_semaphore()

    def greet_ctx(k, carry):
        pl.semaphore_signal(barrier, inc=1, device_id=(d, (c + k) % n_ctx), device_id_type=MESH)
        return carry

    def greet_dp(k, carry):
        pl.semaphore_signal(barrier, inc=1, device_id=((d + k) % n_dp, c), device_id_type=MESH)
        return carry

    lax.fori_loop(1, n_ctx, greet_ctx, 0)
    lax.fori_loop(1, n_dp, greet_dp, 0)

    def remote(src, dst, send, recv, to):
        return pltpu.make_async_remote_copy(
            src_ref=src, dst_ref=dst, send_sem=send, recv_sem=recv, device_id=to, device_id_type=MESH
        )

    def await_bytes(ref, sem):
        pltpu.make_async_copy(ref, ref, sem).wait()

    def exchange(src, dst, phase):
        def body(k, carry):
            zz = k // 2
            away = ((zz + 1) // 2) * (2 * (zz % 2) - 1)
            to = 2 * ((z + away + n_z) % n_z) + (x + k) % 2
            remote(src.at[to], dst.at[c], send_sem.at[phase], recv_sem.at[phase], (d, to)).start()
            return carry

        lax.fori_loop(1, n_ctx, body, 0)
        dst[c] = src[c]

    def exchanged(dst, phase):
        await_bytes(dst.at[pl.ds(0, n_ctx - 1)], recv_sem.at[phase])

    def exchange_sent(src, phase):
        await_bytes(src.at[pl.ds(0, n_ctx - 1)], send_sem.at[phase])

    def spread_dp(ref, place, phase):
        def body(k, carry):
            to = (d + k) % n_dp
            part = ref.at[pl.ds(place, 2)]
            remote(part, part, send_sem.at[phase], recv_sem.at[phase], (to, c)).start()
            return carry

        lax.fori_loop(1, n_dp, body, 0)

    def turned(values):
        return values.T.reshape(n_ctx, group, length)

    loads[0].wait()
    filt_s[...] = turned(taps[...])
    loads[1].wait()
    loads[2].wait()
    for b in range(blocks):
        rows = pl.ds(b * block, block)
        alive = live[0, b].astype(F32)
        key[0, rows] = key[0, rows] * alive.astype(BF16)
    gated_s[...] = turned((key[0].astype(F32) * val[0].astype(F32)).astype(BF16))

    pl.semaphore_wait(barrier, n_ctx - 1 + n_dp - 1)

    def filt_copy(side, to):
        return remote(filt_s.at[to], filt_r.at[c], small_sem.at[0, side], small_sem.at[1, side], (d, to))

    filt_other = filt_copy(1, 2 * pair_out + 1 - x)
    filt_same = filt_copy(0, 2 * pair_out + x)
    filt_other.start()

    @pl.when(shift != 0)
    def _():
        filt_same.start()

    @pl.when(shift == 0)
    def _():
        filt_r[c] = filt_s[c]

    exchange(gated_s, gated_r, 0)

    loads[3].wait()
    loads[4].wait()
    back_s[...] = turned((cot[0].astype(F32) * gate[0].astype(F32)).astype(BF16))
    exchange(back_s, back_r, 1)

    filt_other.wait_recv()

    @pl.when(shift != 0)
    def _():
        filt_same.wait_recv()

    spread_dp(filt_r, 2 * pair_in, 2)
    for load in loads[5:]:
        load.wait()

    low_groups = []
    per = -(-n_low // (3 if n_low % 3 == 0 else 2))
    for start in range(0, n_low, per):
        low_groups.append((start, min(start + per, n_low)))

    def rotate(real, imag, lo, hi, sign):
        shape = (hi - lo, group // 8, 8, length)
        cosv = tcos[lo:hi][:, None]
        sinv = tsin[lo:hi][:, None]
        real, imag = real.reshape(shape), imag.reshape(shape)
        if sign > 0:
            out = (real * cosv - imag * sinv, real * sinv + imag * cosv)
        else:
            out = (real * cosv + imag * sinv, imag * cosv - real * sinv)
        return tuple(part.reshape((hi - lo) * group, length) for part in out)

    real_rows = n_low * group

    def forward(src, spec):
        signal = src[...].reshape(chans, length)
        for lo, hi in low_groups:
            real = jnp.dot(first[lo * group : hi * group], signal, preferred_element_type=F32)
            ilo, ihi = max(lo, 1), min(hi, n_low - 1)
            at = real_rows + (ilo - 1) * group
            imag = jnp.dot(first[at : at + (ihi - ilo) * group], signal, preferred_element_type=F32)
            parts = [imag]
            if lo == 0:
                parts = [jnp.zeros((group, length), F32)] + parts
            if hi == n_low:
                parts = parts + [jnp.zeros((group, length), F32)]
            imag = jnp.concatenate(parts, axis=0) if len(parts) > 1 else imag
            real, imag = rotate(real, imag, lo, hi, -1)
            pair = jnp.concatenate([real.astype(BF16), imag.astype(BF16)], axis=1)
            spec[lo * group : hi * group] = jnp.dot(pair, fwd[...], preferred_element_type=F32)

    def restore(left, right, conjugate, dst, scale):
        for lo, hi in low_groups:
            rows = slice(lo * group, hi * group)
            lr, li = left[rows, :length], left[rows, length:]
            rr, ri = right[rows, :length], right[rows, length:]
            if conjugate:
                real, imag = lr * rr + li * ri, li * rr - lr * ri
            else:
                real, imag = lr * rr - li * ri, lr * ri + li * rr
            pair = jnp.concatenate([real.astype(BF16), imag.astype(BF16)], axis=1)
            both = jnp.dot(pair, inv[...], preferred_element_type=F32)
            real, imag = rotate(both[:, :length], both[:, length:], lo, hi, 1)
            twisted[rows] = real.astype(BF16)
            ilo, ihi = max(lo, 1), min(hi, n_low - 1)
            at = real_rows + (ilo - 1) * group
            twisted[at : at + (ihi - ilo) * group] = imag[(ilo - lo) * group : (ihi - lo) * group].astype(BF16)
        rows_half = chans // 2
        for part in range(2):
            rows = slice(part * rows_half, (part + 1) * rows_half)
            signal = jnp.dot(last[rows], twisted[...], preferred_element_type=F32)
            dst[part * n_z : (part + 1) * n_z] = (signal * scale).astype(BF16).reshape(n_z, group, length)

    inv_len = 1.0 / (2 * n_ctx * length)
    await_bytes(filt_r.at[pl.ds(0, 2 * (n_dp - 1))], recv_sem.at[2])
    forward(filt_r, spec_h)
    exchanged(gated_r, 0)
    forward(gated_r, spec_f)
    restore(spec_f, spec_h, False, conv_s, inv_len)
    exchange(conv_s, conv_r, 3)

    exchanged(back_r, 1)
    forward(back_r, spec_b)
    restore(spec_b, spec_f, True, taps_s, inv_len)

    def share(k, carry):
        to = (d + k) % n_dp
        at = 2 * ((z + shift_of(to)) % n_z)
        remote(taps_s.at[pl.ds(at, 2)], sums_r.at[d], send_sem.at[4], recv_sem.at[4], (to, c)).start()
        return carry

    lax.fori_loop(1, n_dp, share, 0)
    sums_r[d] = taps_s[pl.ds(2 * pair_in, 2)]

    restore(spec_b, spec_h, True, grad_s, inv_len)
    exchange(grad_s, grad_r, 5)

    await_bytes(sums_r.at[pl.ds(0, n_dp - 1)], recv_sem.at[4])
    taps_scale = 1.0 / math.sqrt(n_dp * n_ctx * length)
    summed = sums_r[0].astype(F32)
    for i in range(1, n_dp):
        summed = summed + sums_r[i].astype(F32)
    total[...] = (summed * taps_scale).astype(BF16)

    def taps_copy(side, at):
        return remote(total.at[at], taps_r.at[c], small_sem.at[2, side], small_sem.at[3, side], (d, 2 * pair_in + at))

    taps_other = taps_copy(1, 1 - x)
    taps_same = taps_copy(0, x)
    taps_other.start()

    @pl.when(shift != 0)
    def _():
        taps_same.start()

    @pl.when(shift == 0)
    def _():
        taps_r[c] = total[x]

    def tokens(ref):
        return ref[...].reshape(chans, length).T.astype(F32)

    exchanged(conv_r, 3)
    out_gate[0] = (cot[0].astype(F32) * tokens(conv_r)).astype(BF16)

    taps_other.wait_recv()

    @pl.when(shift != 0)
    def _():
        taps_same.wait_recv()

    spread_dp(taps_r, 2 * pair_out, 6)
    await_bytes(taps_r.at[pl.ds(0, 2 * (n_dp - 1))], recv_sem.at[6])
    out_taps[...] = taps_r[...].reshape(chans, length).T

    exchanged(grad_r, 5)
    grad = tokens(grad_r)
    for b in range(blocks):
        rows = slice(b * block, (b + 1) * block)
        alive = live[0, b].astype(F32)
        out_key[0, rows] = (grad[rows] * val[0, rows].astype(F32) * alive).astype(BF16)
        out_val[0, rows] = (grad[rows] * key[0, rows].astype(F32) * alive).astype(BF16)

    filt_other.wait_send()
    taps_other.wait_send()

    @pl.when(shift != 0)
    def _():
        filt_same.wait_send()
        taps_same.wait_send()

    for src, phase in ((gated_s, 0), (back_s, 1), (conv_s, 3), (grad_s, 5)):
        exchange_sent(src, phase)
    for ref, phase in ((filt_r, 2), (taps_s, 4), (taps_r, 6)):
        await_bytes(ref.at[pl.ds(0, 2 * (n_dp - 1))], send_sem.at[phase])


def local(out_gate, key_gate, value_input, filter_taps, cotangent, block_live):
    n_dp, n_ctx = lax.axis_size("dp"), lax.axis_size("ctx")
    length, chans = key_gate.shape[1:]
    group = chans // n_ctx
    consts = tables(n_ctx, length, group)
    any_spec = pl.BlockSpec(memory_space=pl.ANY)
    signal = (1, length, chans)
    chunks = pltpu.VMEM((n_ctx, group, length), BF16)
    rows = (n_ctx + 1) * group
    scratch = (
        [pltpu.VMEM(signal, BF16)] * 2
        + [pltpu.VMEM(signal[1:], BF16)]
        + [pltpu.VMEM(signal, BF16)] * 2
        + [pltpu.VMEM(t.shape, F32 if t.dtype == np.float32 else BF16) for t in consts]
        + [chunks] * 11
        + [pltpu.VMEM((n_dp, 2, group, length), BF16), pltpu.VMEM((2, group, length), BF16), chunks]
        + [pltpu.VMEM((rows, 2 * length), F32)] * 3
        + [pltpu.VMEM((2 * n_ctx * group, length), BF16)]
        + [
            pltpu.SemaphoreType.DMA((11,)),
            pltpu.SemaphoreType.DMA((7,)),
            pltpu.SemaphoreType.DMA((7,)),
            pltpu.SemaphoreType.DMA((4, 2)),
        ]
    )
    vmem_spec = pl.BlockSpec(memory_space=pltpu.VMEM)
    call = pl.pallas_call(
        functools.partial(kernel, (n_dp, n_ctx)),
        out_shape=[jax.ShapeDtypeStruct(signal, BF16)] * 3 + [jax.ShapeDtypeStruct(signal[1:], BF16)],
        in_specs=[pl.BlockSpec(memory_space=pltpu.SMEM)] + [any_spec] * 11,
        out_specs=[vmem_spec] * 4,
        scratch_shapes=scratch,
        compiler_params=pltpu.CompilerParams(collective_id=0, has_side_effects=True, vmem_limit_bytes=48 * 1024 * 1024),
        cost_estimate=pl.CostEstimate(flops=3_300_000_000, bytes_accessed=6_000_000, transcendentals=0),
    )
    return tuple(call(block_live, key_gate, value_input, filter_taps, cotangent, out_gate, *map(jnp.asarray, consts)))


def solution(mesh):
    spec = P("dp", "ctx", None)
    return jax.shard_map(
        local,
        mesh=mesh,
        in_specs=(spec, spec, spec, P("ctx", None), spec, P("dp", "ctx")),
        out_specs=(spec, spec, spec, P("ctx", None)),
        check_vma=False,
    )
```

```python
import functools
import math

import jax
import jax.numpy as jnp
import ml_dtypes
import numpy as np
from jax import lax
from jax.experimental import pallas as pl
from jax.experimental.pallas import tpu as pltpu
from jax.sharding import PartitionSpec as P

MESH = pl.DeviceIdType.MESH
F32 = jnp.float32
BF16 = jnp.bfloat16


@functools.lru_cache(maxsize=None)
def tables(parts, length, group):
    full = 2 * parts
    low = np.arange(parts + 1)
    block = np.arange(parts)
    step = np.arange(length)
    turn = 2.0 * np.pi / full * (low[:, None] * block[None, :] % full)
    eye = np.eye(group)
    spread = lambda m: np.kron(m, eye)
    cos1, sin1 = np.cos(turn), np.sin(turn)
    first = np.concatenate([spread(cos1), spread(-sin1[1:parts])], axis=0)
    weight = np.full((parts + 1, 1), 2.0)
    weight[0] = weight[parts] = 1.0
    last = np.concatenate([spread((weight * cos1).T), spread((-weight * sin1)[1:parts].T)], axis=1)
    cols = 2.0 * np.pi / length * (step[:, None] * step[None, :] % length)
    cos2, sin2 = np.cos(cols), np.sin(cols)
    fwd = np.block([[cos2, -sin2], [sin2, cos2]])
    inv = np.block([[cos2, sin2], [-sin2, cos2]])
    twist = 2.0 * np.pi / (full * length) * (low[:, None] * step[None, :])
    rows = lambda m: np.repeat(m[:, None, :], 8, axis=1).astype(np.float32)
    half = lambda m: m.astype(np.float32).astype(ml_dtypes.bfloat16)
    return (half(first), half(fwd), half(inv), half(last), rows(np.cos(twist)), rows(np.sin(twist)))


def kernel(
    devices,
    live,
    key_hbm,
    val_hbm,
    taps_hbm,
    cot_hbm,
    gate_hbm,
    first_hbm,
    fwd_hbm,
    inv_hbm,
    last_hbm,
    tcos_hbm,
    tsin_hbm,
    gate_out,
    key_out,
    val_out,
    taps_out,
    key,
    val,
    taps,
    cot,
    gate,
    first,
    fwd,
    inv,
    last,
    tcos,
    tsin,
    gated_s,
    back_s,
    filt_s,
    gated_r,
    back_r,
    filt_r,
    conv_s,
    grad_s,
    taps_s,
    conv_r,
    grad_r,
    sums_r,
    total,
    taps_r,
    spec_f,
    spec_b,
    spec_h,
    twisted,
    out_gate,
    out_key,
    out_val,
    out_taps,
    load_sem,
    send_sem,
    recv_sem,
    small_sem,
    block_sem,
    store_sem,
):
    n_dp, n_ctx = devices
    n_z = n_ctx // 2
    d = lax.axis_index("dp")
    c = lax.axis_index("ctx")
    z, x = c // 2, c % 2
    chans, length = n_ctx * gated_s.shape[1], gated_s.shape[2]
    group = gated_s.shape[1]
    n_low = n_ctx + 1
    n_blocks = max(1, chans // 128)
    per_block, wide = n_ctx // n_blocks, chans // n_blocks
    blocks = live.shape[1]
    block = length // blocks

    def shift_of(place):
        pair, core = place // 2, place % 2
        return pair + core * (n_dp - 2 * pair - (n_dp // 2) * ((n_dp - pair) // n_dp))

    shift = shift_of(d)
    pair_in = (z + shift) % n_z
    pair_out = (z - shift + n_z) % n_z

    loads = [
        pltpu.make_async_copy(src, dst, load_sem.at[i])
        for i, (src, dst) in enumerate(
            [
                (taps_hbm, taps),
                (key_hbm, key),
                (val_hbm, val),
                (cot_hbm, cot),
                (gate_hbm, gate),
                (first_hbm, first),
                (tcos_hbm, tcos),
                (tsin_hbm, tsin),
                (fwd_hbm, fwd),
                (inv_hbm, inv),
                (last_hbm, last),
            ]
        )
    ]
    for load in loads:
        load.start()

    barrier = pltpu.get_barrier_semaphore()

    def greet_ctx(k, carry):
        pl.semaphore_signal(barrier, inc=1, device_id=(d, (c + k) % n_ctx), device_id_type=MESH)
        return carry

    def greet_dp(k, carry):
        pl.semaphore_signal(barrier, inc=1, device_id=((d + k) % n_dp, c), device_id_type=MESH)
        return carry

    lax.fori_loop(1, n_ctx, greet_ctx, 0)
    lax.fori_loop(1, n_dp, greet_dp, 0)

    def remote(src, dst, send, recv, to):
        return pltpu.make_async_remote_copy(
            src_ref=src, dst_ref=dst, send_sem=send, recv_sem=recv, device_id=to, device_id_type=MESH
        )

    def await_bytes(ref, sem):
        pltpu.make_async_copy(ref, ref, sem).wait()

    def exchange(src, dst, phase, sem_of=None, start=1, stop=None):
        recv = recv_sem.at[phase] if sem_of is None else sem_of

        def body(k, carry):
            far = n_ctx - k
            zz = far // 2
            away = ((zz + 1) // 2) * (2 * (zz % 2) - 1)
            to = 2 * ((z + away + n_z) % n_z) + (x + far) % 2
            remote(src.at[to], dst.at[c], send_sem.at[phase], recv, (d, to)).start()
            return carry

        lax.fori_loop(start, n_ctx if stop is None else stop, body, 0)
        if start == 1:
            dst[c] = src[c]

    def exchanged(dst, phase):
        await_bytes(dst.at[pl.ds(0, n_ctx - 1)], recv_sem.at[phase])

    def exchange_sent(src, phase):
        await_bytes(src.at[pl.ds(0, n_ctx - 1)], send_sem.at[phase])

    def spread_dp(ref, place, phase):
        def body(k, carry):
            to = (d + k) % n_dp
            part = ref.at[pl.ds(place, 2)]
            remote(part, part, send_sem.at[phase], recv_sem.at[phase], (to, c)).start()
            return carry

        lax.fori_loop(1, n_dp, body, 0)

    def turned(values):
        return values.T.reshape(n_ctx, group, length)

    loads[0].wait()
    filt_s[...] = turned(taps[...])
    loads[1].wait()
    loads[2].wait()
    for b in range(blocks):
        rows = pl.ds(b * block, block)
        alive = live[0, b].astype(F32)
        key[0, rows] = key[0, rows] * alive.astype(BF16)
    gated_s[...] = turned((key[0].astype(F32) * val[0].astype(F32)).astype(BF16))

    pl.semaphore_wait(barrier, n_ctx - 1 + n_dp - 1)

    def filt_copy(side, to):
        return remote(filt_s.at[to], filt_r.at[c], small_sem.at[0, side], small_sem.at[1, side], (d, to))

    filt_other = filt_copy(1, 2 * pair_out + 1 - x)
    filt_same = filt_copy(0, 2 * pair_out + x)
    filt_other.start()

    @pl.when(shift != 0)
    def _():
        filt_same.start()

    @pl.when(shift == 0)
    def _():
        filt_r[c] = filt_s[c]

    exchange(gated_s, gated_r, 0)

    loads[3].wait()
    loads[4].wait()
    back_s[...] = turned((cot[0].astype(F32) * gate[0].astype(F32)).astype(BF16))
    exchange(back_s, back_r, 1)

    filt_other.wait_recv()

    @pl.when(shift != 0)
    def _():
        filt_same.wait_recv()

    spread_dp(filt_r, 2 * pair_in, 2)
    for load in loads[5:]:
        load.wait()

    low_groups = []
    per = -(-n_low // (3 if n_low % 3 == 0 else 2))
    for start in range(0, n_low, per):
        low_groups.append((start, min(start + per, n_low)))

    def rotate(real, imag, lo, hi, sign):
        shape = (hi - lo, group // 8, 8, length)
        cosv = tcos[lo:hi][:, None]
        sinv = tsin[lo:hi][:, None]
        real, imag = real.reshape(shape), imag.reshape(shape)
        if sign > 0:
            out = (real * cosv - imag * sinv, real * sinv + imag * cosv)
        else:
            out = (real * cosv + imag * sinv, imag * cosv - real * sinv)
        return tuple(part.reshape((hi - lo) * group, length) for part in out)

    real_rows = n_low * group

    def forward(src, spec):
        signal = src[...].reshape(chans, length)
        for lo, hi in low_groups:
            real = jnp.dot(first[lo * group : hi * group], signal, preferred_element_type=F32)
            ilo, ihi = max(lo, 1), min(hi, n_low - 1)
            at = real_rows + (ilo - 1) * group
            imag = jnp.dot(first[at : at + (ihi - ilo) * group], signal, preferred_element_type=F32)
            parts = [imag]
            if lo == 0:
                parts = [jnp.zeros((group, length), F32)] + parts
            if hi == n_low:
                parts = parts + [jnp.zeros((group, length), F32)]
            imag = jnp.concatenate(parts, axis=0) if len(parts) > 1 else imag
            real, imag = rotate(real, imag, lo, hi, -1)
            pair = jnp.concatenate([real.astype(BF16), imag.astype(BF16)], axis=1)
            spec[lo * group : hi * group] = jnp.dot(pair, fwd[...], preferred_element_type=F32)

    def restore(left, right, conjugate, dst, scale):
        for lo, hi in low_groups:
            rows = slice(lo * group, hi * group)
            lr, li = left[rows, :length], left[rows, length:]
            rr, ri = right[rows, :length], right[rows, length:]
            if conjugate:
                real, imag = lr * rr + li * ri, li * rr - lr * ri
            else:
                real, imag = lr * rr - li * ri, lr * ri + li * rr
            pair = jnp.concatenate([real.astype(BF16), imag.astype(BF16)], axis=1)
            both = jnp.dot(pair, inv[...], preferred_element_type=F32)
            real, imag = rotate(both[:, :length], both[:, length:], lo, hi, 1)
            twisted[rows] = real.astype(BF16)
            ilo, ihi = max(lo, 1), min(hi, n_low - 1)
            at = real_rows + (ilo - 1) * group
            twisted[at : at + (ihi - ilo) * group] = imag[(ilo - lo) * group : (ihi - lo) * group].astype(BF16)
        rows_half = chans // 2
        for part in range(2):
            rows = slice(part * rows_half, (part + 1) * rows_half)
            signal = jnp.dot(last[rows], twisted[...], preferred_element_type=F32)
            dst[part * n_z : (part + 1) * n_z] = (signal * scale).astype(BF16).reshape(n_z, group, length)

    inv_len = 1.0 / (2 * n_ctx * length)
    await_bytes(filt_r.at[pl.ds(0, 2 * (n_dp - 1))], recv_sem.at[2])
    forward(filt_r, spec_h)
    exchanged(gated_r, 0)
    forward(gated_r, spec_f)
    restore(spec_f, spec_h, False, conv_s, inv_len)
    exchange(conv_s, conv_r, 3)

    exchanged(back_r, 1)
    forward(back_r, spec_b)
    restore(spec_b, spec_f, True, taps_s, inv_len)

    def share(k, carry):
        to = (d + k) % n_dp
        at = 2 * ((z + shift_of(to)) % n_z)
        remote(taps_s.at[pl.ds(at, 2)], sums_r.at[d], send_sem.at[4], recv_sem.at[4], (to, c)).start()
        return carry

    lax.fori_loop(1, n_dp, share, 0)
    sums_r[d] = taps_s[pl.ds(2 * pair_in, 2)]

    restore(spec_b, spec_h, True, grad_s, inv_len)
    ahead = 1 + n_ctx // 5
    exchange(grad_s, grad_r, 5, block_sem.at[c // per_block], 1, ahead)

    await_bytes(sums_r.at[pl.ds(0, n_dp - 1)], recv_sem.at[4])
    taps_scale = 1.0 / math.sqrt(n_dp * n_ctx * length)
    summed = sums_r[0].astype(F32)
    for i in range(1, n_dp):
        summed = summed + sums_r[i].astype(F32)
    total[...] = (summed * taps_scale).astype(BF16)

    def taps_copy(side, at):
        return remote(total.at[at], taps_r.at[c], small_sem.at[2, side], small_sem.at[3, side], (d, 2 * pair_in + at))

    taps_other = taps_copy(1, 1 - x)
    taps_same = taps_copy(0, x)
    taps_other.start()

    @pl.when(shift != 0)
    def _():
        taps_same.start()

    @pl.when(shift == 0)
    def _():
        taps_r[c] = total[x]

    exchange(grad_s, grad_r, 5, block_sem.at[c // per_block], ahead)

    def tokens(values):
        return values.reshape(-1, length).T.astype(F32)

    stores = []

    def store(src, dst):
        stores.append(pltpu.make_async_copy(src, dst, store_sem.at[len(stores)]))
        stores[-1].start()

    exchanged(conv_r, 3)
    out_gate[0] = (cot[0].astype(F32) * tokens(conv_r[...])).astype(BF16)
    store(out_gate, gate_out)

    taps_other.wait_recv()

    @pl.when(shift != 0)
    def _():
        taps_same.wait_recv()

    spread_dp(taps_r, 2 * pair_out, 6)
    await_bytes(taps_r.at[pl.ds(0, 2 * (n_dp - 1))], recv_sem.at[6])
    out_taps[...] = taps_r[...].reshape(chans, length).T
    store(out_taps, taps_out)

    order = sorted(range(n_blocks), key=lambda r: -min(r, n_blocks - r))
    for rel in order:
        at = (c // per_block + rel) % n_blocks
        await_bytes(grad_r.at[pl.ds(0, per_block - (rel == 0))], block_sem.at[at])
        grad = tokens(grad_r[pl.ds(at * per_block, per_block)])
        lanes = pl.ds(pl.multiple_of(at * wide, wide), wide)
        for b in range(blocks):
            rows = slice(b * block, (b + 1) * block)
            alive = live[0, b].astype(F32)
            out_key[0, rows, lanes] = (grad[rows] * val[0, rows, lanes].astype(F32) * alive).astype(BF16)
            out_val[0, rows, lanes] = (grad[rows] * key[0, rows, lanes].astype(F32) * alive).astype(BF16)
        store(out_key.at[:, :, lanes], key_out.at[:, :, lanes])
        store(out_val.at[:, :, lanes], val_out.at[:, :, lanes])

    filt_other.wait_send()
    taps_other.wait_send()

    @pl.when(shift != 0)
    def _():
        filt_same.wait_send()
        taps_same.wait_send()

    for src, phase in ((gated_s, 0), (back_s, 1), (conv_s, 3), (grad_s, 5)):
        exchange_sent(src, phase)
    for ref, phase in ((filt_r, 2), (taps_s, 4), (taps_r, 6)):
        await_bytes(ref.at[pl.ds(0, 2 * (n_dp - 1))], send_sem.at[phase])
    for copy in stores:
        copy.wait()


def copy_kernel(*refs):
    count = (len(refs) - 2) // 3
    sources, targets, stages = refs[:count], refs[count : 2 * count], refs[2 * count : 3 * count]
    load_sem, store_sem = refs[3 * count :]
    loads = [pltpu.make_async_copy(sources[i], stages[i], load_sem.at[i]) for i in range(count)]
    stores = [pltpu.make_async_copy(stages[i], targets[i], store_sem.at[i]) for i in range(count)]
    for load in loads:
        load.start()
    for load, store in zip(loads, stores):
        load.wait()
        store.start()
    for store in stores:
        store.wait()


def local(out_gate, key_gate, value_input, filter_taps, cotangent, block_live):
    n_dp, n_ctx = lax.axis_size("dp"), lax.axis_size("ctx")
    length, chans = key_gate.shape[1:]
    group = chans // n_ctx
    consts = tables(n_ctx, length, group)
    hbm_spec = pl.BlockSpec(memory_space=pltpu.HBM)
    signal = (1, length, chans)
    chunks = pltpu.VMEM((n_ctx, group, length), BF16)
    rows = (n_ctx + 1) * group
    n_blocks = max(1, chans // 128)
    scratch = (
        [pltpu.VMEM(signal, BF16)] * 2
        + [pltpu.VMEM(signal[1:], BF16)]
        + [pltpu.VMEM(signal, BF16)] * 2
        + [pltpu.VMEM(t.shape, F32 if t.dtype == np.float32 else BF16) for t in consts]
        + [chunks] * 11
        + [pltpu.VMEM((n_dp, 2, group, length), BF16), pltpu.VMEM((2, group, length), BF16), chunks]
        + [pltpu.VMEM((rows, 2 * length), F32)] * 3
        + [pltpu.VMEM((2 * n_ctx * group, length), BF16)]
        + [pltpu.VMEM(signal, BF16)] * 3
        + [pltpu.VMEM(signal[1:], BF16)]
        + [
            pltpu.SemaphoreType.DMA((11,)),
            pltpu.SemaphoreType.DMA((7,)),
            pltpu.SemaphoreType.DMA((7,)),
            pltpu.SemaphoreType.DMA((4, 2)),
            pltpu.SemaphoreType.DMA((n_blocks,)),
            pltpu.SemaphoreType.DMA((2 + 2 * n_blocks,)),
        ]
    )
    out_shape = [jax.ShapeDtypeStruct(signal, BF16)] * 3 + [jax.ShapeDtypeStruct(signal[1:], BF16)]
    call = pl.pallas_call(
        functools.partial(kernel, (n_dp, n_ctx)),
        out_shape=out_shape,
        in_specs=[pl.BlockSpec(memory_space=pltpu.SMEM)] + [hbm_spec] * 11,
        out_specs=[hbm_spec] * 4,
        scratch_shapes=scratch,
        compiler_params=pltpu.CompilerParams(collective_id=0, has_side_effects=True, vmem_limit_bytes=60 * 1024 * 1024),
        cost_estimate=pl.CostEstimate(flops=3_300_000_000, bytes_accessed=6_000_000, transcendentals=0),
    )
    results = call(block_live, key_gate, value_input, filter_taps, cotangent, out_gate, *map(jnp.asarray, consts))
    final = pl.pallas_call(
        copy_kernel,
        out_shape=out_shape,
        in_specs=[hbm_spec] * 4,
        out_specs=[hbm_spec] * 4,
        scratch_shapes=[pltpu.VMEM(o.shape, BF16) for o in out_shape] + [pltpu.SemaphoreType.DMA((4,))] * 2,
        cost_estimate=pl.CostEstimate(flops=0, bytes_accessed=2_000_000, transcendentals=0),
    )
    return tuple(final(*results))


def solution(mesh):
    spec = P("dp", "ctx", None)
    return jax.shard_map(
        local,
        mesh=mesh,
        in_specs=(spec, spec, spec, P("ctx", None), spec, P("dp", "ctx")),
        out_specs=(spec, spec, spec, P("ctx", None)),
        check_vma=False,
    )
```

```python
import functools
import math

import jax
import jax.numpy as jnp
import ml_dtypes
import numpy as np
from jax import lax
from jax.experimental import pallas as pl
from jax.experimental.pallas import tpu as pltpu
from jax.sharding import PartitionSpec as P

MESH = pl.DeviceIdType.MESH
F32 = jnp.float32
BF16 = jnp.bfloat16


@functools.lru_cache(maxsize=None)
def tables(parts, length, group):
    full = 2 * parts
    low = np.arange(parts + 1)
    block = np.arange(parts)
    step = np.arange(length)
    turn = 2.0 * np.pi / full * (low[:, None] * block[None, :] % full)
    eye = np.eye(group)
    spread = lambda m: np.kron(m, eye)
    cos1, sin1 = np.cos(turn), np.sin(turn)
    first = np.concatenate([spread(cos1), spread(-sin1[1:parts])], axis=0)
    weight = np.full((parts + 1, 1), 2.0)
    weight[0] = weight[parts] = 1.0
    last = np.concatenate([spread((weight * cos1).T), spread((-weight * sin1)[1:parts].T)], axis=1)
    cols = 2.0 * np.pi / length * (step[:, None] * step[None, :] % length)
    cos2, sin2 = np.cos(cols), np.sin(cols)
    fwd = np.block([[cos2, -sin2], [sin2, cos2]])
    inv = np.block([[cos2, sin2], [-sin2, cos2]])
    twist = 2.0 * np.pi / (full * length) * (low[:, None] * step[None, :])
    rows = lambda m: np.repeat(m[:, None, :], 8, axis=1).astype(np.float32)
    half = lambda m: m.astype(np.float32).astype(ml_dtypes.bfloat16)
    return (half(first), half(fwd), half(inv), half(last), rows(np.cos(twist)), rows(np.sin(twist)))


def kernel(
    devices,
    live,
    key_hbm,
    val_hbm,
    taps_hbm,
    cot_hbm,
    gate_hbm,
    first_hbm,
    fwd_hbm,
    inv_hbm,
    last_hbm,
    tcos_hbm,
    tsin_hbm,
    gate_out,
    key_out,
    val_out,
    shared,
    key,
    val,
    taps,
    cot,
    gate,
    first,
    fwd,
    inv,
    last,
    tcos,
    tsin,
    gated_s,
    back_s,
    filt_s,
    gated_r,
    back_r,
    filt_r,
    conv_s,
    grad_s,
    taps_s,
    conv_r,
    grad_r,
    sums_r,
    total,
    taps_r,
    spec_f,
    spec_b,
    spec_h,
    twisted,
    out_gate,
    out_key,
    out_val,
    load_sem,
    send_sem,
    recv_sem,
    small_sem,
    block_sem,
    store_sem,
):
    n_dp, n_ctx = devices
    n_z = n_ctx // 2
    d = lax.axis_index("dp")
    c = lax.axis_index("ctx")
    z, x = c // 2, c % 2
    chans, length = n_ctx * gated_s.shape[1], gated_s.shape[2]
    group = gated_s.shape[1]
    n_low = n_ctx + 1
    n_blocks = max(1, chans // 128)
    per_block, wide = n_ctx // n_blocks, chans // n_blocks
    blocks = live.shape[1]
    block = length // blocks

    def shift_of(place):
        pair, core = place // 2, place % 2
        return pair + core * (n_dp - 2 * pair - (n_dp // 2) * ((n_dp - pair) // n_dp))

    shift = shift_of(d)
    pair_in = (z + shift) % n_z
    pair_out = (z - shift + n_z) % n_z

    loads = [
        pltpu.make_async_copy(src, dst, load_sem.at[i])
        for i, (src, dst) in enumerate(
            [
                (taps_hbm, taps),
                (key_hbm, key),
                (val_hbm, val),
                (cot_hbm, cot),
                (gate_hbm, gate),
                (first_hbm, first),
                (tcos_hbm, tcos),
                (tsin_hbm, tsin),
                (fwd_hbm, fwd),
                (inv_hbm, inv),
                (last_hbm, last),
            ]
        )
    ]
    for load in loads:
        load.start()

    barrier = pltpu.get_barrier_semaphore()

    def greet_ctx(k, carry):
        pl.semaphore_signal(barrier, inc=1, device_id=(d, (c + k) % n_ctx), device_id_type=MESH)
        return carry

    def greet_dp(k, carry):
        pl.semaphore_signal(barrier, inc=1, device_id=((d + k) % n_dp, c), device_id_type=MESH)
        return carry

    lax.fori_loop(1, n_ctx, greet_ctx, 0)
    lax.fori_loop(1, n_dp, greet_dp, 0)

    def remote(src, dst, send, recv, to):
        return pltpu.make_async_remote_copy(
            src_ref=src, dst_ref=dst, send_sem=send, recv_sem=recv, device_id=to, device_id_type=MESH
        )

    def await_bytes(ref, sem):
        pltpu.make_async_copy(ref, ref, sem).wait()

    def exchange(src, dst, phase, sem_of=None, start=1, stop=None):
        recv = recv_sem.at[phase] if sem_of is None else sem_of

        def body(k, carry):
            far = n_ctx - k
            zz = far // 2
            away = ((zz + 1) // 2) * (2 * (zz % 2) - 1)
            to = 2 * ((z + away + n_z) % n_z) + (x + far) % 2
            remote(src.at[to], dst.at[c], send_sem.at[phase], recv, (d, to)).start()
            return carry

        lax.fori_loop(start, n_ctx if stop is None else stop, body, 0)
        if start == 1:
            dst[c] = src[c]

    def exchanged(dst, phase):
        await_bytes(dst.at[pl.ds(0, n_ctx - 1)], recv_sem.at[phase])

    def exchange_sent(src, phase):
        await_bytes(src.at[pl.ds(0, n_ctx - 1)], send_sem.at[phase])

    def spread_dp(ref, dst, place, phase):
        def body(k, carry):
            to = (d + k) % n_dp
            part = pl.ds(place, 2)
            remote(ref.at[part], dst.at[part], send_sem.at[phase], recv_sem.at[phase], (to, c)).start()
            return carry

        lax.fori_loop(1, n_dp, body, 0)

    def turned(values):
        return values.T.reshape(n_ctx, group, length)

    loads[0].wait()
    filt_s[...] = turned(taps[...])
    loads[1].wait()
    loads[2].wait()
    for b in range(blocks):
        rows = pl.ds(b * block, block)
        alive = live[0, b].astype(F32)
        key[0, rows] = key[0, rows] * alive.astype(BF16)
    gated_s[...] = turned((key[0].astype(F32) * val[0].astype(F32)).astype(BF16))

    pl.semaphore_wait(barrier, n_ctx - 1 + n_dp - 1)

    def filt_copy(side, to):
        return remote(filt_s.at[to], filt_r.at[c], small_sem.at[0, side], small_sem.at[1, side], (d, to))

    filt_other = filt_copy(1, 2 * pair_out + 1 - x)
    filt_same = filt_copy(0, 2 * pair_out + x)
    filt_other.start()

    @pl.when(shift != 0)
    def _():
        filt_same.start()

    @pl.when(shift == 0)
    def _():
        filt_r[c] = filt_s[c]

    exchange(gated_s, gated_r, 0)

    loads[3].wait()
    loads[4].wait()
    back_s[...] = turned((cot[0].astype(F32) * gate[0].astype(F32)).astype(BF16))
    exchange(back_s, back_r, 1)

    filt_other.wait_recv()

    @pl.when(shift != 0)
    def _():
        filt_same.wait_recv()

    spread_dp(filt_r, filt_r, 2 * pair_in, 2)
    for load in loads[5:]:
        load.wait()

    low_groups = []
    per = -(-n_low // (3 if n_low % 3 == 0 else 2))
    for start in range(0, n_low, per):
        low_groups.append((start, min(start + per, n_low)))

    def rotate(real, imag, lo, hi, sign):
        shape = (hi - lo, group // 8, 8, length)
        cosv = tcos[lo:hi][:, None]
        sinv = tsin[lo:hi][:, None]
        real, imag = real.reshape(shape), imag.reshape(shape)
        if sign > 0:
            out = (real * cosv - imag * sinv, real * sinv + imag * cosv)
        else:
            out = (real * cosv + imag * sinv, imag * cosv - real * sinv)
        return tuple(part.reshape((hi - lo) * group, length) for part in out)

    real_rows = n_low * group

    def forward(src, spec):
        signal = src[...].reshape(chans, length)
        for lo, hi in low_groups:
            real = jnp.dot(first[lo * group : hi * group], signal, preferred_element_type=F32)
            ilo, ihi = max(lo, 1), min(hi, n_low - 1)
            at = real_rows + (ilo - 1) * group
            imag = jnp.dot(first[at : at + (ihi - ilo) * group], signal, preferred_element_type=F32)
            parts = [imag]
            if lo == 0:
                parts = [jnp.zeros((group, length), F32)] + parts
            if hi == n_low:
                parts = parts + [jnp.zeros((group, length), F32)]
            imag = jnp.concatenate(parts, axis=0) if len(parts) > 1 else imag
            real, imag = rotate(real, imag, lo, hi, -1)
            pair = jnp.concatenate([real.astype(BF16), imag.astype(BF16)], axis=1)
            spec[lo * group : hi * group] = jnp.dot(pair, fwd[...], preferred_element_type=F32)

    def restore(left, right, conjugate, dst, scale):
        for lo, hi in low_groups:
            rows = slice(lo * group, hi * group)
            lr, li = left[rows, :length], left[rows, length:]
            rr, ri = right[rows, :length], right[rows, length:]
            if conjugate:
                real, imag = lr * rr + li * ri, li * rr - lr * ri
            else:
                real, imag = lr * rr - li * ri, lr * ri + li * rr
            pair = jnp.concatenate([real.astype(BF16), imag.astype(BF16)], axis=1)
            both = jnp.dot(pair, inv[...], preferred_element_type=F32)
            real, imag = rotate(both[:, :length], both[:, length:], lo, hi, 1)
            twisted[rows] = real.astype(BF16)
            ilo, ihi = max(lo, 1), min(hi, n_low - 1)
            at = real_rows + (ilo - 1) * group
            twisted[at : at + (ihi - ilo) * group] = imag[(ilo - lo) * group : (ihi - lo) * group].astype(BF16)
        rows_half = chans // 2
        for part in range(2):
            rows = slice(part * rows_half, (part + 1) * rows_half)
            signal = jnp.dot(last[rows], twisted[...], preferred_element_type=F32)
            dst[part * n_z : (part + 1) * n_z] = (signal * scale).astype(BF16).reshape(n_z, group, length)

    inv_len = 1.0 / (2 * n_ctx * length)
    await_bytes(filt_r.at[pl.ds(0, 2 * (n_dp - 1))], recv_sem.at[2])
    forward(filt_r, spec_h)
    exchanged(gated_r, 0)
    forward(gated_r, spec_f)
    restore(spec_f, spec_h, False, conv_s, inv_len)
    exchange(conv_s, conv_r, 3)

    exchanged(back_r, 1)
    forward(back_r, spec_b)
    restore(spec_b, spec_f, True, taps_s, inv_len)

    def share(k, carry):
        to = (d + k) % n_dp
        at = 2 * ((z + shift_of(to)) % n_z)
        remote(taps_s.at[pl.ds(at, 2)], sums_r.at[d], send_sem.at[4], recv_sem.at[4], (to, c)).start()
        return carry

    lax.fori_loop(1, n_dp, share, 0)
    sums_r[d] = taps_s[pl.ds(2 * pair_in, 2)]

    restore(spec_b, spec_h, True, grad_s, inv_len)
    ahead = 1 + n_ctx // 5
    exchange(grad_s, grad_r, 5, block_sem.at[c // per_block], 1, ahead)

    await_bytes(sums_r.at[pl.ds(0, n_dp - 1)], recv_sem.at[4])
    taps_scale = 1.0 / math.sqrt(n_dp * n_ctx * length)
    summed = sums_r[0].astype(F32)
    for i in range(1, n_dp):
        summed = summed + sums_r[i].astype(F32)
    total[...] = (summed * taps_scale).astype(BF16)

    def taps_copy(side, at):
        return remote(total.at[at], taps_r.at[c], small_sem.at[2, side], small_sem.at[3, side], (d, 2 * pair_in + at))

    taps_other = taps_copy(1, 1 - x)
    taps_same = taps_copy(0, x)
    taps_other.start()

    @pl.when(shift != 0)
    def _():
        taps_same.start()

    @pl.when(shift == 0)
    def _():
        taps_r[c] = total[x]

    exchange(grad_s, grad_r, 5, block_sem.at[c // per_block], ahead)

    def tokens(values):
        return values.reshape(-1, length).T.astype(F32)

    stores = []

    def store(src, dst):
        stores.append(pltpu.make_async_copy(src, dst, store_sem.at[len(stores)]))
        stores[-1].start()

    exchanged(conv_r, 3)
    out_gate[0] = (cot[0].astype(F32) * tokens(conv_r[...])).astype(BF16)
    store(out_gate, gate_out)

    taps_other.wait_recv()

    @pl.when(shift != 0)
    def _():
        taps_same.wait_recv()

    mine = pl.ds(2 * pair_out, 2)
    store(taps_r.at[mine], shared.at[mine])
    spread_dp(taps_r, shared, 2 * pair_out, 6)
    order = sorted(range(n_blocks), key=lambda r: -min(r, n_blocks - r))
    for rel in order:
        at = (c // per_block + rel) % n_blocks
        await_bytes(grad_r.at[pl.ds(0, per_block - (rel == 0))], block_sem.at[at])
        grad = tokens(grad_r[pl.ds(at * per_block, per_block)])
        lanes = pl.ds(pl.multiple_of(at * wide, wide), wide)
        for b in range(blocks):
            rows = slice(b * block, (b + 1) * block)
            alive = live[0, b].astype(F32)
            out_key[0, rows, lanes] = (grad[rows] * val[0, rows, lanes].astype(F32) * alive).astype(BF16)
            out_val[0, rows, lanes] = (grad[rows] * key[0, rows, lanes].astype(F32) * alive).astype(BF16)
        store(out_key.at[:, :, lanes], key_out.at[:, :, lanes])
        store(out_val.at[:, :, lanes], val_out.at[:, :, lanes])

    await_bytes(shared.at[pl.ds(0, 2 * (n_dp - 1))], recv_sem.at[6])

    filt_other.wait_send()
    taps_other.wait_send()

    @pl.when(shift != 0)
    def _():
        filt_same.wait_send()
        taps_same.wait_send()

    for src, phase in ((gated_s, 0), (back_s, 1), (conv_s, 3), (grad_s, 5)):
        exchange_sent(src, phase)
    for ref, phase in ((filt_r, 2), (taps_s, 4), (taps_r, 6)):
        await_bytes(ref.at[pl.ds(0, 2 * (n_dp - 1))], send_sem.at[phase])
    for copy in stores:
        copy.wait()


def finish(gate, key, val, shared, gate_out, key_out, val_out, taps_out, gate_v, key_v, val_v, shared_v, taps_v, load_sem, store_sem):
    pairs = [(shared, shared_v), (gate, gate_v), (key, key_v), (val, val_v)]
    loads = [pltpu.make_async_copy(src, dst, load_sem.at[i]) for i, (src, dst) in enumerate(pairs)]
    pairs = [(taps_v, taps_out), (gate_v, gate_out), (key_v, key_out), (val_v, val_out)]
    stores = [pltpu.make_async_copy(src, dst, store_sem.at[i]) for i, (src, dst) in enumerate(pairs)]
    for load in loads:
        load.start()
    loads[0].wait()
    taps_v[...] = shared_v[...].reshape(-1, shared_v.shape[2]).T
    stores[0].start()
    for load, store in zip(loads[1:], stores[1:]):
        load.wait()
        store.start()
    for store in stores:
        store.wait()


def local(out_gate, key_gate, value_input, filter_taps, cotangent, block_live):
    n_dp, n_ctx = lax.axis_size("dp"), lax.axis_size("ctx")
    length, chans = key_gate.shape[1:]
    group = chans // n_ctx
    consts = tables(n_ctx, length, group)
    hbm_spec = pl.BlockSpec(memory_space=pltpu.HBM)
    signal = (1, length, chans)
    chunks = pltpu.VMEM((n_ctx, group, length), BF16)
    rows = (n_ctx + 1) * group
    n_blocks = max(1, chans // 128)
    scratch = (
        [pltpu.VMEM(signal, BF16)] * 2
        + [pltpu.VMEM(signal[1:], BF16)]
        + [pltpu.VMEM(signal, BF16)] * 2
        + [pltpu.VMEM(t.shape, F32 if t.dtype == np.float32 else BF16) for t in consts]
        + [chunks] * 11
        + [pltpu.VMEM((n_dp, 2, group, length), BF16), pltpu.VMEM((2, group, length), BF16), chunks]
        + [pltpu.VMEM((rows, 2 * length), F32)] * 3
        + [pltpu.VMEM((2 * n_ctx * group, length), BF16)]
        + [pltpu.VMEM(signal, BF16)] * 3
        + [
            pltpu.SemaphoreType.DMA((11,)),
            pltpu.SemaphoreType.DMA((7,)),
            pltpu.SemaphoreType.DMA((7,)),
            pltpu.SemaphoreType.DMA((4, 2)),
            pltpu.SemaphoreType.DMA((n_blocks,)),
            pltpu.SemaphoreType.DMA((2 + 2 * n_blocks,)),
        ]
    )
    out_shape = [jax.ShapeDtypeStruct(signal, BF16)] * 3 + [jax.ShapeDtypeStruct(signal[1:], BF16)]
    call = pl.pallas_call(
        functools.partial(kernel, (n_dp, n_ctx)),
        out_shape=out_shape[:3] + [jax.ShapeDtypeStruct(chunks.shape, BF16)],
        in_specs=[pl.BlockSpec(memory_space=pltpu.SMEM)] + [hbm_spec] * 11,
        out_specs=[hbm_spec] * 4,
        scratch_shapes=scratch,
        compiler_params=pltpu.CompilerParams(collective_id=0, has_side_effects=True, vmem_limit_bytes=60 * 1024 * 1024),
        cost_estimate=pl.CostEstimate(flops=3_300_000_000, bytes_accessed=6_000_000, transcendentals=0),
    )
    results = call(block_live, key_gate, value_input, filter_taps, cotangent, out_gate, *map(jnp.asarray, consts))
    final = pl.pallas_call(
        finish,
        out_shape=out_shape,
        in_specs=[hbm_spec] * 4,
        out_specs=[hbm_spec] * 4,
        scratch_shapes=[pltpu.VMEM(signal, BF16)] * 3
        + [chunks, pltpu.VMEM(signal[1:], BF16)]
        + [pltpu.SemaphoreType.DMA((4,))] * 2,
        cost_estimate=pl.CostEstimate(flops=0, bytes_accessed=2_000_000, transcendentals=0),
    )
    return tuple(final(*results))


def solution(mesh):
    spec = P("dp", "ctx", None)
    return jax.shard_map(
        local,
        mesh=mesh,
        in_specs=(spec, spec, spec, P("ctx", None), spec, P("dp", "ctx")),
        out_specs=(spec, spec, spec, P("ctx", None)),
        check_vma=False,
    )
```

```python
import functools
import math

import jax
import jax.numpy as jnp
import ml_dtypes
import numpy as np
from jax import lax
from jax.experimental import pallas as pl
from jax.experimental.pallas import tpu as pltpu
from jax.sharding import PartitionSpec as P

MESH = pl.DeviceIdType.MESH
F32 = jnp.float32
BF16 = jnp.bfloat16


@functools.lru_cache(maxsize=None)
def tables(parts, length, group):
    full = 2 * parts
    low = np.arange(parts + 1)
    block = np.arange(parts)
    step = np.arange(length)
    turn = 2.0 * np.pi / full * (low[:, None] * block[None, :] % full)
    eye = np.eye(group)
    spread = lambda m: np.kron(m, eye)
    cos1, sin1 = np.cos(turn), np.sin(turn)
    first = np.concatenate([spread(cos1), spread(-sin1[1:parts])], axis=0)
    weight = np.full((parts + 1, 1), 2.0)
    weight[0] = weight[parts] = 1.0
    last = np.concatenate([spread((weight * cos1).T), spread((-weight * sin1)[1:parts].T)], axis=1)
    cols = 2.0 * np.pi / length * (step[:, None] * step[None, :] % length)
    cos2, sin2 = np.cos(cols), np.sin(cols)
    fwd = np.block([[cos2, -sin2], [sin2, cos2]])
    inv = np.block([[cos2, sin2], [-sin2, cos2]])
    twist = 2.0 * np.pi / (full * length) * (low[:, None] * step[None, :])
    rows = lambda m: np.repeat(m[:, None, :], 8, axis=1).astype(np.float32)
    half = lambda m: m.astype(np.float32).astype(ml_dtypes.bfloat16)
    return (half(first), half(fwd), half(inv), half(last), rows(np.cos(twist)), rows(np.sin(twist)))


def kernel(
    devices,
    live,
    key_hbm,
    val_hbm,
    taps_hbm,
    cot_hbm,
    gate_hbm,
    first_hbm,
    fwd_hbm,
    inv_hbm,
    last_hbm,
    tcos_hbm,
    tsin_hbm,
    gate_out,
    key_out,
    val_out,
    shared,
    key,
    val,
    taps,
    cot,
    gate,
    first,
    fwd,
    inv,
    last,
    tcos,
    tsin,
    gated_s,
    back_s,
    filt_s,
    gated_r,
    back_r,
    filt_r,
    conv_s,
    grad_s,
    taps_s,
    conv_r,
    grad_r,
    sums_r,
    total,
    taps_r,
    spec_f,
    spec_b,
    spec_h,
    twisted,
    out_gate,
    out_key,
    out_val,
    load_sem,
    send_sem,
    recv_sem,
    small_sem,
    block_sem,
    store_sem,
):
    n_dp, n_ctx = devices
    n_z = n_ctx // 2
    d = lax.axis_index("dp")
    c = lax.axis_index("ctx")
    z, x = c // 2, c % 2
    chans, length = n_ctx * gated_s.shape[1], gated_s.shape[2]
    group = gated_s.shape[1]
    n_low = n_ctx + 1
    n_blocks = max(1, chans // 128)
    per_block, wide = n_ctx // n_blocks, chans // n_blocks
    blocks = live.shape[1]
    block = length // blocks

    def shift_of(place):
        pair, core = place // 2, place % 2
        return pair + core * (n_dp - 2 * pair - (n_dp // 2) * ((n_dp - pair) // n_dp))

    shift = shift_of(d)
    pair_in = (z + shift) % n_z
    pair_out = (z - shift + n_z) % n_z

    loads = [
        pltpu.make_async_copy(src, dst, load_sem.at[i])
        for i, (src, dst) in enumerate(
            [
                (taps_hbm, taps),
                (key_hbm, key),
                (val_hbm, val),
                (cot_hbm, cot),
                (gate_hbm, gate),
                (first_hbm, first),
                (tcos_hbm, tcos),
                (tsin_hbm, tsin),
                (fwd_hbm, fwd),
                (inv_hbm, inv),
                (last_hbm, last),
            ]
        )
    ]
    for load in loads:
        load.start()

    barrier = pltpu.get_barrier_semaphore()

    def greet_ctx(k, carry):
        pl.semaphore_signal(barrier, inc=1, device_id=(d, (c + k) % n_ctx), device_id_type=MESH)
        return carry

    def greet_dp(k, carry):
        pl.semaphore_signal(barrier, inc=1, device_id=((d + k) % n_dp, c), device_id_type=MESH)
        return carry

    lax.fori_loop(1, n_ctx, greet_ctx, 0)
    lax.fori_loop(1, n_dp, greet_dp, 0)

    def remote(src, dst, send, recv, to):
        return pltpu.make_async_remote_copy(
            src_ref=src, dst_ref=dst, send_sem=send, recv_sem=recv, device_id=to, device_id_type=MESH
        )

    def await_bytes(ref, sem):
        pltpu.make_async_copy(ref, ref, sem).wait()

    def exchange(src, dst, phase, sem_of=None, start=1, stop=None):
        recv = recv_sem.at[phase] if sem_of is None else sem_of

        def body(k, carry):
            far = n_ctx - k
            zz = far // 2
            away = ((zz + 1) // 2) * (2 * (zz % 2) - 1)
            to = 2 * ((z + away + n_z) % n_z) + (x + far) % 2
            remote(src.at[to], dst.at[c], send_sem.at[phase], recv, (d, to)).start()
            return carry

        lax.fori_loop(start, n_ctx if stop is None else stop, body, 0)
        if start == 1:
            dst[c] = src[c]

    def exchanged(dst, phase):
        await_bytes(dst.at[pl.ds(0, n_ctx - 1)], recv_sem.at[phase])

    def exchange_sent(src, phase):
        await_bytes(src.at[pl.ds(0, n_ctx - 1)], send_sem.at[phase])

    def spread_dp(ref, dst, place, phase):
        def body(k, carry):
            to = (d + k) % n_dp
            part = pl.ds(place, 2)
            remote(ref.at[part], dst.at[part], send_sem.at[phase], recv_sem.at[phase], (to, c)).start()
            return carry

        lax.fori_loop(1, n_dp, body, 0)

    def turned(values):
        return values.T.reshape(n_ctx, group, length)

    loads[0].wait()
    filt_s[...] = turned(taps[...])
    loads[1].wait()
    loads[2].wait()
    for b in range(blocks):
        rows = pl.ds(b * block, block)
        alive = live[0, b].astype(F32)
        key[0, rows] = key[0, rows] * alive.astype(BF16)
    gated_s[...] = turned((key[0].astype(F32) * val[0].astype(F32)).astype(BF16))

    pl.semaphore_wait(barrier, n_ctx - 1 + n_dp - 1)

    def filt_copy(side, to):
        return remote(filt_s.at[to], filt_r.at[c], small_sem.at[0, side], small_sem.at[1, side], (d, to))

    filt_other = filt_copy(1, 2 * pair_out + 1 - x)
    filt_same = filt_copy(0, 2 * pair_out + x)
    filt_other.start()

    @pl.when(shift != 0)
    def _():
        filt_same.start()

    @pl.when(shift == 0)
    def _():
        filt_r[c] = filt_s[c]

    exchange(gated_s, gated_r, 0)

    loads[3].wait()
    loads[4].wait()
    back_s[...] = turned((cot[0].astype(F32) * gate[0].astype(F32)).astype(BF16))
    exchange(back_s, back_r, 1)

    filt_other.wait_recv()

    @pl.when(shift != 0)
    def _():
        filt_same.wait_recv()

    spread_dp(filt_r, filt_r, 2 * pair_in, 2)
    for load in loads[5:]:
        load.wait()

    low_groups = []
    per = -(-n_low // (3 if n_low % 3 == 0 else 2))
    for start in range(0, n_low, per):
        low_groups.append((start, min(start + per, n_low)))

    def rotate(real, imag, lo, hi, sign):
        shape = (hi - lo, group // 8, 8, length)
        cosv = tcos[lo:hi][:, None]
        sinv = tsin[lo:hi][:, None]
        real, imag = real.reshape(shape), imag.reshape(shape)
        if sign > 0:
            out = (real * cosv - imag * sinv, real * sinv + imag * cosv)
        else:
            out = (real * cosv + imag * sinv, imag * cosv - real * sinv)
        return tuple(part.reshape((hi - lo) * group, length) for part in out)

    real_rows = n_low * group

    def forward(src, spec):
        signal = src[...].reshape(chans, length)
        for lo, hi in low_groups:
            real = jnp.dot(first[lo * group : hi * group], signal, preferred_element_type=F32)
            ilo, ihi = max(lo, 1), min(hi, n_low - 1)
            at = real_rows + (ilo - 1) * group
            imag = jnp.dot(first[at : at + (ihi - ilo) * group], signal, preferred_element_type=F32)
            parts = [imag]
            if lo == 0:
                parts = [jnp.zeros((group, length), F32)] + parts
            if hi == n_low:
                parts = parts + [jnp.zeros((group, length), F32)]
            imag = jnp.concatenate(parts, axis=0) if len(parts) > 1 else imag
            real, imag = rotate(real, imag, lo, hi, -1)
            pair = jnp.concatenate([real.astype(BF16), imag.astype(BF16)], axis=1)
            spec[lo * group : hi * group] = jnp.dot(pair, fwd[...], preferred_element_type=F32)

    def restore(left, right, conjugate, dst, scale):
        for lo, hi in low_groups:
            rows = slice(lo * group, hi * group)
            lr, li = left[rows, :length], left[rows, length:]
            rr, ri = right[rows, :length], right[rows, length:]
            if conjugate:
                real, imag = lr * rr + li * ri, li * rr - lr * ri
            else:
                real, imag = lr * rr - li * ri, lr * ri + li * rr
            pair = jnp.concatenate([real.astype(BF16), imag.astype(BF16)], axis=1)
            both = jnp.dot(pair, inv[...], preferred_element_type=F32)
            real, imag = rotate(both[:, :length], both[:, length:], lo, hi, 1)
            twisted[rows] = real.astype(BF16)
            ilo, ihi = max(lo, 1), min(hi, n_low - 1)
            at = real_rows + (ilo - 1) * group
            twisted[at : at + (ihi - ilo) * group] = imag[(ilo - lo) * group : (ihi - lo) * group].astype(BF16)
        rows_half = chans // 2
        for part in range(2):
            rows = slice(part * rows_half, (part + 1) * rows_half)
            signal = jnp.dot(last[rows], twisted[...], preferred_element_type=F32)
            dst[part * n_z : (part + 1) * n_z] = (signal * scale).astype(BF16).reshape(n_z, group, length)

    inv_len = 1.0 / (2 * n_ctx * length)
    await_bytes(filt_r.at[pl.ds(0, 2 * (n_dp - 1))], recv_sem.at[2])
    forward(filt_r, spec_h)
    exchanged(gated_r, 0)
    forward(gated_r, spec_f)
    restore(spec_f, spec_h, False, conv_s, inv_len)
    exchange(conv_s, conv_r, 3)

    exchanged(back_r, 1)
    forward(back_r, spec_b)
    restore(spec_b, spec_f, True, taps_s, inv_len)

    def share(k, carry):
        to = (d + k) % n_dp
        at = 2 * ((z + shift_of(to)) % n_z)
        remote(taps_s.at[pl.ds(at, 2)], sums_r.at[d], send_sem.at[4], recv_sem.at[4], (to, c)).start()
        return carry

    lax.fori_loop(1, n_dp, share, 0)
    sums_r[d] = taps_s[pl.ds(2 * pair_in, 2)]

    restore(spec_b, spec_h, True, grad_s, inv_len)
    ahead = 1 + n_ctx // 5
    exchange(grad_s, grad_r, 5, block_sem.at[c // per_block], 1, ahead)

    await_bytes(sums_r.at[pl.ds(0, n_dp - 1)], recv_sem.at[4])
    taps_scale = 1.0 / math.sqrt(n_dp * n_ctx * length)
    summed = sums_r[0].astype(F32)
    for i in range(1, n_dp):
        summed = summed + sums_r[i].astype(F32)
    total[...] = (summed * taps_scale).astype(BF16)

    def taps_copy(side, at):
        return remote(total.at[at], taps_r.at[c], small_sem.at[2, side], small_sem.at[3, side], (d, 2 * pair_in + at))

    taps_other = taps_copy(1, 1 - x)
    taps_same = taps_copy(0, x)
    taps_other.start()

    @pl.when(shift != 0)
    def _():
        taps_same.start()

    @pl.when(shift == 0)
    def _():
        taps_r[c] = total[x]

    exchange(grad_s, grad_r, 5, block_sem.at[c // per_block], ahead)

    def tokens(values):
        return values.reshape(-1, length).T.astype(F32)

    stores = []

    def store(src, dst):
        stores.append(pltpu.make_async_copy(src, dst, store_sem.at[len(stores)]))
        stores[-1].start()

    taps_other.wait_recv()

    @pl.when(shift != 0)
    def _():
        taps_same.wait_recv()

    mine = pl.ds(2 * pair_out, 2)
    store(taps_r.at[mine], shared.at[mine])
    spread_dp(taps_r, shared, 2 * pair_out, 6)

    exchanged(conv_r, 3)
    out_gate[0] = (cot[0].astype(F32) * tokens(conv_r[...])).astype(BF16)
    store(out_gate, gate_out)
    order = sorted(range(n_blocks), key=lambda r: -min(r, n_blocks - r))
    for rel in order:
        at = (c // per_block + rel) % n_blocks
        await_bytes(grad_r.at[pl.ds(0, per_block - (rel == 0))], block_sem.at[at])
        grad = tokens(grad_r[pl.ds(at * per_block, per_block)])
        lanes = pl.ds(pl.multiple_of(at * wide, wide), wide)
        for b in range(blocks):
            rows = slice(b * block, (b + 1) * block)
            alive = live[0, b].astype(F32)
            out_key[0, rows, lanes] = (grad[rows] * val[0, rows, lanes].astype(F32) * alive).astype(BF16)
            out_val[0, rows, lanes] = (grad[rows] * key[0, rows, lanes].astype(F32) * alive).astype(BF16)
        store(out_key.at[:, :, lanes], key_out.at[:, :, lanes])
        store(out_val.at[:, :, lanes], val_out.at[:, :, lanes])

    await_bytes(shared.at[pl.ds(0, 2 * (n_dp - 1))], recv_sem.at[6])

    filt_other.wait_send()
    taps_other.wait_send()

    @pl.when(shift != 0)
    def _():
        filt_same.wait_send()
        taps_same.wait_send()

    for src, phase in ((gated_s, 0), (back_s, 1), (conv_s, 3), (grad_s, 5)):
        exchange_sent(src, phase)
    for ref, phase in ((filt_r, 2), (taps_s, 4), (taps_r, 6)):
        await_bytes(ref.at[pl.ds(0, 2 * (n_dp - 1))], send_sem.at[phase])
    for copy in stores:
        copy.wait()


def finish(gate, key, val, shared, gate_out, key_out, val_out, taps_out, gate_v, key_v, val_v, shared_v, taps_v, load_sem, store_sem):
    pairs = [(shared, shared_v), (gate, gate_v), (key, key_v), (val, val_v)]
    loads = [pltpu.make_async_copy(src, dst, load_sem.at[i]) for i, (src, dst) in enumerate(pairs)]
    pairs = [(taps_v, taps_out), (gate_v, gate_out), (key_v, key_out), (val_v, val_out)]
    stores = [pltpu.make_async_copy(src, dst, store_sem.at[i]) for i, (src, dst) in enumerate(pairs)]
    for load in loads:
        load.start()
    loads[0].wait()
    taps_v[...] = shared_v[...].reshape(-1, shared_v.shape[2]).T
    stores[0].start()
    for load, store in zip(loads[1:], stores[1:]):
        load.wait()
        store.start()
    for store in stores:
        store.wait()


def local(out_gate, key_gate, value_input, filter_taps, cotangent, block_live):
    n_dp, n_ctx = lax.axis_size("dp"), lax.axis_size("ctx")
    length, chans = key_gate.shape[1:]
    group = chans // n_ctx
    consts = tables(n_ctx, length, group)
    hbm_spec = pl.BlockSpec(memory_space=pltpu.HBM)
    signal = (1, length, chans)
    chunks = pltpu.VMEM((n_ctx, group, length), BF16)
    rows = (n_ctx + 1) * group
    n_blocks = max(1, chans // 128)
    scratch = (
        [pltpu.VMEM(signal, BF16)] * 2
        + [pltpu.VMEM(signal[1:], BF16)]
        + [pltpu.VMEM(signal, BF16)] * 2
        + [pltpu.VMEM(t.shape, F32 if t.dtype == np.float32 else BF16) for t in consts]
        + [chunks] * 11
        + [pltpu.VMEM((n_dp, 2, group, length), BF16), pltpu.VMEM((2, group, length), BF16), chunks]
        + [pltpu.VMEM((rows, 2 * length), F32)] * 3
        + [pltpu.VMEM((2 * n_ctx * group, length), BF16)]
        + [pltpu.VMEM(signal, BF16)] * 3
        + [
            pltpu.SemaphoreType.DMA((11,)),
            pltpu.SemaphoreType.DMA((7,)),
            pltpu.SemaphoreType.DMA((7,)),
            pltpu.SemaphoreType.DMA((4, 2)),
            pltpu.SemaphoreType.DMA((n_blocks,)),
            pltpu.SemaphoreType.DMA((2 + 2 * n_blocks,)),
        ]
    )
    out_shape = [jax.ShapeDtypeStruct(signal, BF16)] * 3 + [jax.ShapeDtypeStruct(signal[1:], BF16)]
    call = pl.pallas_call(
        functools.partial(kernel, (n_dp, n_ctx)),
        out_shape=out_shape[:3] + [jax.ShapeDtypeStruct(chunks.shape, BF16)],
        in_specs=[pl.BlockSpec(memory_space=pltpu.SMEM)] + [hbm_spec] * 11,
        out_specs=[hbm_spec] * 4,
        scratch_shapes=scratch,
        compiler_params=pltpu.CompilerParams(collective_id=0, has_side_effects=True, vmem_limit_bytes=60 * 1024 * 1024),
        cost_estimate=pl.CostEstimate(flops=3_300_000_000, bytes_accessed=6_000_000, transcendentals=0),
    )
    results = call(block_live, key_gate, value_input, filter_taps, cotangent, out_gate, *map(jnp.asarray, consts))
    final = pl.pallas_call(
        finish,
        out_shape=out_shape,
        in_specs=[hbm_spec] * 4,
        out_specs=[hbm_spec] * 4,
        scratch_shapes=[pltpu.VMEM(signal, BF16)] * 3
        + [chunks, pltpu.VMEM(signal[1:], BF16)]
        + [pltpu.SemaphoreType.DMA((4,))] * 2,
        cost_estimate=pl.CostEstimate(flops=0, bytes_accessed=2_000_000, transcendentals=0),
    )
    return tuple(final(*results))


def solution(mesh):
    spec = P("dp", "ctx", None)
    return jax.shard_map(
        local,
        mesh=mesh,
        in_specs=(spec, spec, spec, P("ctx", None), spec, P("dp", "ctx")),
        out_specs=(spec, spec, spec, P("ctx", None)),
        check_vma=False,
    )
```
